32 devices in a mesh: space: 8 (over y, x, core), chan: 4 (over z).
Axes of the slice: x: 2, y: 2, z: 4, core: 2. Of those that a mesh axis runs over, the one named last changes fastest.
Arguments:
- voxels: bfloat16 [32, 16, 16, 512], P(None, 'space'), may hold values from -6 to 6
- first_filters: bfloat16 [3, 3, 3, 64, 32], P(None, None, None, 'chan'), may hold values from -0.21875 to 0.21875
- second_filters: bfloat16 [3, 3, 3, 64, 64], P(None, None, None, 'chan'), may hold values from -0.15625 to 0.15625
Outputs:
- filtered: bfloat16 [64, 16, 16, 512], P('chan', 'space')
The draws below stay inside these ranges and needn't reach their ends.
All inputs are finite; a program needn't handle non-finite values.
Results may differ from the reference program's by a relative error of at most 0.0049.
Values may be sent and summed in bfloat16 or wider, within the bound.
A program may use at most 64 MiB of HBM per device.

```python
import jax
import jax.numpy as jnp
from jax import lax

C_IN = 32
C_MID = 64
C_OUT = 64
GH = 8
TD = 2
TH = 16
W = 512
TILE_ROWS = 16
N_SPACE = 8


def block_scale(own_key, dims, cuts, smallest, high):
    def one(position, parts):
        steps = jax.random.uniform(jax.random.fold_in(jax.random.fold_in(own_key, 6), position), (parts,), jnp.float32, smallest / len(cuts), high / len(cuts))
        return jnp.repeat(jnp.exp(steps), dims[position] // parts).reshape((-1,) + (1,) * (len(dims) - position - 1))

    level = one(*cuts[0])
    for cut in cuts[1:]:
        level = level * one(*cut)
    return level


def scatter_about(key, extent, width, bound, shards=(), dtype=jnp.bfloat16):
    gain = block_scale(key, extent, shards, -0.22, 0.18) if shards else 1.0
    drawn = jax.random.normal(key, extent, jnp.float32) * width * gain
    return jnp.minimum(jnp.maximum(drawn, -bound), bound).astype(dtype)


def setup_inputs(seed: int = 0) -> dict:
    key_list = jax.random.split(jax.random.key(seed), 4)
    return {
        "voxels": scatter_about(key_list[0], (C_IN, TILE_ROWS, TH, W), 1.0, 6.0, ((1, 8),)),
        "first_filters": scatter_about(key_list[1], (3, 3, 3, C_MID, C_IN), (27 * C_IN) ** -0.5, 0.21875, ((3, 4),)),
        "second_filters": scatter_about(key_list[2], (3, 3, 3, C_OUT, C_MID), (27 * C_MID) ** -0.5, 0.15625, ((3, 4),)),
    }


def to_volume(tile_array):
    channels = tile_array.shape[0]
    grid_depth = N_SPACE // GH
    shaped = tile_array.reshape(channels, N_SPACE, TD, TH, W)
    shaped = jnp.roll(shaped, GH + GH // 4, axis=1)
    shaped = shaped.reshape(channels, grid_depth, GH, TD, TH, W)
    shaped = shaped.transpose(0, 1, 3, 2, 4, 5)
    return shaped.reshape(channels, grid_depth * TD, GH * TH, W)


def to_tiles(volume):
    channels = volume.shape[0]
    grid_depth = N_SPACE // GH
    shaped = volume.reshape(channels, grid_depth, TD, GH, TH, W)
    shaped = shaped.transpose(0, 1, 3, 2, 4, 5)
    shaped = shaped.reshape(channels, N_SPACE, TD, TH, W)
    shaped = jnp.roll(shaped, -(GH + GH // 4), axis=1)
    return shaped.reshape(channels, N_SPACE * TD, TH, W)


def correlate(volume, filters):
    kernel = filters.astype(jnp.float32).transpose(3, 4, 0, 1, 2)
    result = lax.conv_general_dilated(volume.astype(jnp.float32)[None], kernel, (1, 1, 1), "SAME",
                                      dimension_numbers=("NCDHW", "OIDHW", "NCDHW"))
    return result[0]


def reference(voxels, first_filters, second_filters):
    volume = to_volume(voxels)
    hidden = jax.nn.relu(correlate(volume, first_filters)).astype(jnp.bfloat16)
    output = jax.nn.relu(correlate(hidden, second_filters)).astype(jnp.bfloat16)
    return to_tiles(output)
```

```python
import functools

import jax
import jax.numpy as jnp
from jax import lax
from jax.experimental import pallas as pl
from jax.experimental.pallas import tpu as pltpu
from jax.sharding import PartitionSpec as P

GH = 8


def passed_along(value, axis, steps):
    count = lax.axis_size(axis)
    pairs = [(source, (source + steps) % count) for source in range(count)]
    return lax.ppermute(value, axis, pairs)


def extended(value, sides, width):
    for axis, dim in sides:
        size, length = (lax.axis_size(axis), value.shape[dim])
        up = [(i, (i + 1) % size) for i in range(size - 1)]
        down = [(j, i) for i, j in up]
        last = lax.slice_in_dim(value, length - width, length, axis=dim)
        initial = lax.slice_in_dim(value, 0, width, axis=dim)
        before = lax.ppermute(last, axis, up)
        after = lax.ppermute(initial, axis, down)
        value = jnp.concatenate([before, value, after], axis=dim)
    return value


def stack_taps(sided):
    return jnp.concatenate([sided[..., :-2], sided[..., 1:-1], sided[..., 2:]], 0)


def tile_border(volume_tile, above, below, front, back):
    tile_count = lax.axis_size("space")
    position = (lax.axis_index("space") + GH + GH // 4) % tile_count
    tile_row = position % GH
    depth_tile = position // GH
    grid_depth = tile_count // GH
    above_rim = above(volume_tile[:, :, -1:, :])
    below_rim = below(volume_tile[:, :, :1, :])
    above_rim = jnp.where(tile_row > 0, above_rim, jnp.zeros_like(above_rim))
    below_rim = jnp.where(tile_row < GH - 1, below_rim, jnp.zeros_like(below_rim))
    taller = jnp.concatenate([above_rim, volume_tile, below_rim], 2)
    front_rim = front(taller[:, -1:])
    back_rim = back(taller[:, :1])
    front_rim = jnp.where(depth_tile > 0, front_rim, jnp.zeros_like(front_rim))
    back_rim = jnp.where(depth_tile < grid_depth - 1, back_rim, jnp.zeros_like(back_rim))
    return jnp.concatenate([front_rim, taller, back_rim], 1)


def input_above(rim_cells):
    return passed_along(rim_cells, "space", 1)


def input_below(rim_cells):
    return passed_along(rim_cells, "space", -1)


def input_front(rim_cells):
    return passed_along(rim_cells, "space", GH)


def input_back(rim_cells):
    return passed_along(rim_cells, "space", -GH)


def hidden_above(rim_cells):
    return passed_along(rim_cells, "space", 1)


def hidden_below(rim_cells):
    return passed_along(rim_cells, "space", -1)


def hidden_front(rim_cells):
    return passed_along(rim_cells, "space", GH)


def hidden_back(rim_cells):
    return passed_along(rim_cells, "space", -GH)


def correlate(stacked, filters, depth_rows, height_rows):
    out_count = filters.shape[3]
    running = jnp.zeros((out_count, depth_rows, height_rows, stacked.shape[3]), jnp.float32)
    for depth_tap in range(3):
        for height_tap in range(3):
            matrix = filters[depth_tap, height_tap].transpose(1, 0, 2).reshape(out_count, -1)
            window = stacked[
                :, depth_tap : depth_tap + depth_rows, height_tap : height_tap + height_rows, :
            ]
            running = running + jnp.einsum(
                "ok,kdhw->odhw", matrix, window, preferred_element_type=jnp.float32
            )
    return running


def local(voxels, first_filters, second_filters):
    depth_rows = voxels.shape[1]
    height_rows = voxels.shape[2]
    width_cells = voxels.shape[3]
    share = width_cells // lax.axis_size("chan")
    own_cols = lax.dynamic_slice_in_dim(voxels, lax.axis_index("chan") * share, share, 3)
    every_first, every_second = (
        lax.all_gather(first_filters, "chan", axis=3, tiled=True),
        lax.all_gather(second_filters, "chan", axis=3, tiled=True),
    )
    sided = extended(own_cols, (("chan", 3),), 1)
    padded = tile_border(sided, input_above, input_below, input_front, input_back)
    hidden = jax.nn.relu(
        correlate(stack_taps(padded), every_first, depth_rows, height_rows)
    ).astype(jnp.bfloat16)
    hidden_sided = extended(hidden, (("chan", 3),), 1)
    hidden_pad = tile_border(hidden_sided, hidden_above, hidden_below, hidden_front, hidden_back)
    result = jax.nn.relu(
        correlate(stack_taps(hidden_pad), every_second, depth_rows, height_rows)
    ).astype(jnp.bfloat16)
    return lax.all_to_all(result, "chan", split_axis=0, concat_axis=3, tiled=True)


MESH = pl.DeviceIdType.MESH
BF = jnp.bfloat16
F32 = jnp.float32
LANES = 128


def combine_width(product, part):
    lane = lax.broadcasted_iota(jnp.int32, (part, product.shape[1]), 1)
    width = product.shape[1]
    left = jnp.where(lane == 0, 0.0, pltpu.roll(product[:part], 1, 1))
    right = jnp.where(lane == width - 1, 0.0, pltpu.roll(product[2 * part :], width - 1, 1))
    return left + product[part : 2 * part] + right


def tile_kernel(
    sizes, vox_hbm, first_hbm, second_hbm, out_ref,
    vox, first, second, wide, xs, gathered, w1, w2, hid, rows_out,
    load_sem, send_sem, recv_sem,
):
    n_space, n_chan, c_in, own, c_mid, height, width = sizes
    s = lax.axis_index("space")
    c = lax.axis_index("chan")
    below, above = lax.rem(s + 1, n_space), lax.rem(s + n_space - 1, n_space)
    position = lax.rem(s + GH + GH // 4, n_space)

    loads = [
        pltpu.make_async_copy(first_hbm, first, load_sem.at[0]),
        pltpu.make_async_copy(vox_hbm, vox, load_sem.at[1]),
        pltpu.make_async_copy(second_hbm, second, load_sem.at[2]),
    ]
    for load in loads:
        load.start()

    barrier = pltpu.get_barrier_semaphore()
    for neighbour in (below, above):
        pl.semaphore_signal(barrier, inc=1, device_id={"space": neighbour}, device_id_type=MESH)
    for k in range(1, n_chan):
        pl.semaphore_signal(
            barrier, inc=1, device_id={"chan": lax.rem(c + k, n_chan)}, device_id_type=MESH
        )

    loads[0].wait()
    spare = jnp.zeros((own, c_in), BF)
    for e in range(3):
        for a in range(3):
            gathered[c, e * 3 + a] = jnp.concatenate(
                [first[a, 0, e], first[a, 1, e], first[a, 2, e], spare], axis=1
            )
    pl.semaphore_wait(barrier, n_chan + 1)
    copies = []
    for k in range(1, n_chan):
        copy = pltpu.make_async_remote_copy(
            src_ref=gathered.at[c],
            dst_ref=gathered.at[c],
            send_sem=send_sem.at[k - 1],
            recv_sem=recv_sem.at[k - 1],
            device_id={"chan": lax.rem(c + k, n_chan)},
            device_id_type=MESH,
        )
        copy.start()
        copies.append(copy)

    loads[1].wait()
    tiles = width // LANES
    for d in range(2):
        for t in range(tiles):
            part = vox[:, d, :, pl.ds(t * LANES, LANES)].astype(F32)
            wide[d, t] = part.reshape(c_in * height, LANES)

    def turn(h):
        for d in range(2):
            for t in range(tiles):
                xs[d, pl.ds((h + 2) * c_in, c_in), pl.ds(t * LANES, LANES)] = wide[
                    d, t, pl.ds(h, c_in, stride=height), :
                ].astype(BF)

    for h in (0, 1, height - 2, height - 1):
        turn(h)
    halos = []
    for i, (start, landing, target) in enumerate(
        ((height, 0, below), (2, height + 2, above))
    ):
        copy = pltpu.make_async_remote_copy(
            src_ref=xs.at[:, pl.ds(start * c_in, 2 * c_in), :],
            dst_ref=xs.at[:, pl.ds(landing * c_in, 2 * c_in), :],
            send_sem=send_sem.at[n_chan - 1 + i],
            recv_sem=recv_sem.at[n_chan - 1 + i],
            device_id={"space": target},
            device_id_type=MESH,
        )
        copy.start()
        halos.append(copy)
    for h in range(2, height - 2):
        turn(h)
    xs[:, pl.ds((height + 4) * c_in, c_in), :] = jnp.zeros((2, c_in, width), BF)

    loads[2].wait()
    for e in range(3):
        for od in range(2):
            w2[pl.ds((e * 2 + od) * own, own), :] = jnp.concatenate(
                [second[i - od + 1, b, e] for b in range(3) for i in range(2)], axis=1
            )

    for copy in copies:
        copy.wait()
    lanes = 4 * c_in
    for e in range(3):
        for od in range(2):
            for k in range(n_chan):
                at = pl.ds((e * 2 + od) * c_mid + k * own, own)
                for i in range(2):
                    w1[at, pl.ds(i * lanes, lanes)] = gathered[k, e * 3 + i - od + 1]

    def layer_one(r, _=None):
        window = pl.ds(pl.multiple_of(r * c_in, c_in), lanes)
        stacked = jnp.concatenate([xs[0, window, :], xs[1, window, :]], axis=0)
        product = jnp.dot(w1[...], stacked, preferred_element_type=F32)
        row = jnp.maximum(combine_width(product, 2 * c_mid), 0.0).astype(BF)
        hid[pl.ds(pl.multiple_of(r * 2 * c_mid, 2 * c_mid), 2 * c_mid), :] = row

    lax.fori_loop(2, height - 1, lambda r, _: layer_one(r), None)
    for copy in halos:
        copy.wait()

    @pl.when(position == 0)
    def _():
        xs[:, : 2 * c_in, :] = jnp.zeros((2, 2 * c_in, width), BF)

    @pl.when(position == n_space - 1)
    def _():
        xs[:, pl.ds((height + 2) * c_in, 2 * c_in), :] = jnp.zeros((2, 2 * c_in, width), BF)

    lax.fori_loop(0, 2, lambda r, _: layer_one(r), None)
    lax.fori_loop(height - 1, height + 2, lambda r, _: layer_one(r), None)

    @pl.when(position == 0)
    def _():
        hid[: 2 * c_mid, :] = jnp.zeros((2 * c_mid, width), BF)

    @pl.when(position == n_space - 1)
    def _():
        hid[pl.ds((height + 1) * 2 * c_mid, 2 * c_mid), :] = jnp.zeros((2 * c_mid, width), BF)

    def layer_two(r):
        window = pl.ds(pl.multiple_of(r * 2 * c_mid, 2 * c_mid), 6 * c_mid)
        product = jnp.dot(w2[...], hid[window, :], preferred_element_type=F32)
        row = jnp.maximum(combine_width(product, 2 * own), 0.0)
        for d in range(2):
            for t in range(tiles):
                rows_out[d, t, pl.ds(pl.multiple_of(r * own, own), own), :] = row[
                    d * own : (d + 1) * own, t * LANES : (t + 1) * LANES
                ]

    lax.fori_loop(0, height, lambda r, _: layer_two(r), None)
    for d in range(2):
        for o in range(own):
            for t in range(tiles):
                out_ref[o, d, :, pl.ds(t * LANES, LANES)] = rows_out[
                    d, t, pl.ds(o, height, stride=own), :
                ].astype(BF)


def one_layer_of_tiles(voxels, first_filters, second_filters):
    n_space, n_chan = lax.axis_size("space"), lax.axis_size("chan")
    c_in, depth, height, width = voxels.shape
    own, c_mid = second_filters.shape[3:]
    sizes = (n_space, n_chan, c_in, own, c_mid, height, width)
    any_space = pl.BlockSpec(memory_space=pl.ANY)
    return pl.pallas_call(
        functools.partial(tile_kernel, sizes),
        out_shape=jax.ShapeDtypeStruct((own, depth, height, width), BF),
        in_specs=[any_space] * 3,
        out_specs=pl.BlockSpec(memory_space=pltpu.VMEM),
        scratch_shapes=[
            pltpu.VMEM(voxels.shape, BF),
            pltpu.VMEM(first_filters.shape, BF),
            pltpu.VMEM(second_filters.shape, BF),
            pltpu.VMEM((2, width // LANES, c_in * height, LANES), F32),
            pltpu.VMEM((2, (height + 5) * c_in, width), BF),
            pltpu.VMEM((n_chan, 9, own, 4 * c_in), BF),
            pltpu.VMEM((6 * c_mid, 8 * c_in), BF),
            pltpu.VMEM((6 * own, 6 * c_mid), BF),
            pltpu.VMEM(((height + 2) * 2 * c_mid, width), BF),
            pltpu.VMEM((2, width // LANES, height * own, LANES), F32),
            pltpu.SemaphoreType.DMA((3,)),
            pltpu.SemaphoreType.DMA((n_chan + 1,)),
            pltpu.SemaphoreType.DMA((n_chan + 1,)),
        ],
        compiler_params=pltpu.CompilerParams(
            collective_id=0, has_side_effects=True, vmem_limit_bytes=32 * 1024 * 1024
        ),
    )(voxels, first_filters, second_filters)


def solution(mesh):
    return jax.shard_map(
        one_layer_of_tiles if mesh.shape["space"] == GH else local,
        mesh=mesh,
        in_specs=(
            P(None, "space", None, None),
            P(None, None, None, "chan", None),
            P(None, None, None, "chan", None),
        ),
        out_specs=P("chan", "space", None, None),
        check_vma=False,
    )
```

```python
import functools

import jax
import jax.numpy as jnp
from jax import lax
from jax.experimental import pallas as pl
from jax.experimental.pallas import tpu as pltpu
from jax.sharding import PartitionSpec as P

GH = 8


def passed_along(value, axis, steps):
    count = lax.axis_size(axis)
    pairs = [(source, (source + steps) % count) for source in range(count)]
    return lax.ppermute(value, axis, pairs)


def extended(value, sides, width):
    for axis, dim in sides:
        size, length = (lax.axis_size(axis), value.shape[dim])
        up = [(i, (i + 1) % size) for i in range(size - 1)]
        down = [(j, i) for i, j in up]
        last = lax.slice_in_dim(value, length - width, length, axis=dim)
        initial = lax.slice_in_dim(value, 0, width, axis=dim)
        before = lax.ppermute(last, axis, up)
        after = lax.ppermute(initial, axis, down)
        value = jnp.concatenate([before, value, after], axis=dim)
    return value


def stack_taps(sided):
    return jnp.concatenate([sided[..., :-2], sided[..., 1:-1], sided[..., 2:]], 0)


def tile_border(volume_tile, above, below, front, back):
    tile_count = lax.axis_size("space")
    position = (lax.axis_index("space") + GH + GH // 4) % tile_count
    tile_row = position % GH
    depth_tile = position // GH
    grid_depth = tile_count // GH
    above_rim = above(volume_tile[:, :, -1:, :])
    below_rim = below(volume_tile[:, :, :1, :])
    above_rim = jnp.where(tile_row > 0, above_rim, jnp.zeros_like(above_rim))
    below_rim = jnp.where(tile_row < GH - 1, below_rim, jnp.zeros_like(below_rim))
    taller = jnp.concatenate([above_rim, volume_tile, below_rim], 2)
    front_rim = front(taller[:, -1:])
    back_rim = back(taller[:, :1])
    front_rim = jnp.where(depth_tile > 0, front_rim, jnp.zeros_like(front_rim))
    back_rim = jnp.where(depth_tile < grid_depth - 1, back_rim, jnp.zeros_like(back_rim))
    return jnp.concatenate([front_rim, taller, back_rim], 1)


def input_above(rim_cells):
    return passed_along(rim_cells, "space", 1)


def input_below(rim_cells):
    return passed_along(rim_cells, "space", -1)


def input_front(rim_cells):
    return passed_along(rim_cells, "space", GH)


def input_back(rim_cells):
    return passed_along(rim_cells, "space", -GH)


def hidden_above(rim_cells):
    return passed_along(rim_cells, "space", 1)


def hidden_below(rim_cells):
    return passed_along(rim_cells, "space", -1)


def hidden_front(rim_cells):
    return passed_along(rim_cells, "space", GH)


def hidden_back(rim_cells):
    return passed_along(rim_cells, "space", -GH)


def correlate(stacked, filters, depth_rows, height_rows):
    out_count = filters.shape[3]
    running = jnp.zeros((out_count, depth_rows, height_rows, stacked.shape[3]), jnp.float32)
    for depth_tap in range(3):
        for height_tap in range(3):
            matrix = filters[depth_tap, height_tap].transpose(1, 0, 2).reshape(out_count, -1)
            window = stacked[
                :, depth_tap : depth_tap + depth_rows, height_tap : height_tap + height_rows, :
            ]
            running = running + jnp.einsum(
                "ok,kdhw->odhw", matrix, window, preferred_element_type=jnp.float32
            )
    return running


def local(voxels, first_filters, second_filters):
    depth_rows = voxels.shape[1]
    height_rows = voxels.shape[2]
    width_cells = voxels.shape[3]
    share = width_cells // lax.axis_size("chan")
    own_cols = lax.dynamic_slice_in_dim(voxels, lax.axis_index("chan") * share, share, 3)
    every_first, every_second = (
        lax.all_gather(first_filters, "chan", axis=3, tiled=True),
        lax.all_gather(second_filters, "chan", axis=3, tiled=True),
    )
    sided = extended(own_cols, (("chan", 3),), 1)
    padded = tile_border(sided, input_above, input_below, input_front, input_back)
    hidden = jax.nn.relu(
        correlate(stack_taps(padded), every_first, depth_rows, height_rows)
    ).astype(jnp.bfloat16)
    hidden_sided = extended(hidden, (("chan", 3),), 1)
    hidden_pad = tile_border(hidden_sided, hidden_above, hidden_below, hidden_front, hidden_back)
    result = jax.nn.relu(
        correlate(stack_taps(hidden_pad), every_second, depth_rows, height_rows)
    ).astype(jnp.bfloat16)
    return lax.all_to_all(result, "chan", split_axis=0, concat_axis=3, tiled=True)


MESH = pl.DeviceIdType.MESH
BF = jnp.bfloat16
F32 = jnp.float32
LANES = 128


def combine_width(product, part):
    lane = lax.broadcasted_iota(jnp.int32, (part, product.shape[1]), 1)
    width = product.shape[1]
    left = jnp.where(lane == 0, 0.0, pltpu.roll(product[:part], 1, 1))
    right = jnp.where(lane == width - 1, 0.0, pltpu.roll(product[2 * part :], width - 1, 1))
    return left + product[part : 2 * part] + right


def tile_kernel(
    sizes, vox_hbm, first_hbm, second_hbm, out_ref,
    vox, first, second, wide, xs, gathered, w1, w2, hid, rows_out,
    load_sem, send_sem, recv_sem,
):
    n_space, n_chan, c_in, own, c_mid, height, width = sizes
    s = lax.axis_index("space")
    c = lax.axis_index("chan")
    below, above = lax.rem(s + 1, n_space), lax.rem(s + n_space - 1, n_space)
    position = lax.rem(s + GH + GH // 4, n_space)

    loads = [
        pltpu.make_async_copy(first_hbm, first, load_sem.at[0]),
        pltpu.make_async_copy(vox_hbm, vox, load_sem.at[1]),
        pltpu.make_async_copy(second_hbm, second, load_sem.at[2]),
    ]
    for load in loads:
        load.start()

    barrier = pltpu.get_barrier_semaphore()
    for neighbour in (below, above):
        pl.semaphore_signal(barrier, inc=1, device_id={"space": neighbour}, device_id_type=MESH)
    for k in range(1, n_chan):
        pl.semaphore_signal(
            barrier, inc=1, device_id={"chan": lax.rem(c + k, n_chan)}, device_id_type=MESH
        )

    loads[0].wait()
    spare = jnp.zeros((own, c_in), BF)
    for e in range(3):
        for a in range(3):
            gathered[c, e * 3 + a] = jnp.concatenate(
                [first[a, 0, e], first[a, 1, e], first[a, 2, e], spare], axis=1
            )
    loads[1].wait()
    tiles = width // LANES
    for d in range(2):
        for t in range(tiles):
            part = vox[:, d, :, pl.ds(t * LANES, LANES)].astype(F32)
            wide[d, t] = part.reshape(c_in * height, LANES)

    def turn(h):
        for d in range(2):
            for t in range(tiles):
                xs[d, pl.ds((h + 2) * c_in, c_in), pl.ds(t * LANES, LANES)] = wide[
                    d, t, pl.ds(h, c_in, stride=height), :
                ].astype(BF)

    for h in (0, 1, height - 2, height - 1):
        turn(h)

    pl.semaphore_wait(barrier, n_chan + 1)
    copies = []
    for k in range(1, n_chan):
        copy = pltpu.make_async_remote_copy(
            src_ref=gathered.at[c],
            dst_ref=gathered.at[c],
            send_sem=send_sem.at[k - 1],
            recv_sem=recv_sem.at[k - 1],
            device_id={"chan": lax.rem(c + k, n_chan)},
            device_id_type=MESH,
        )
        copy.start()
        copies.append(copy)
    halos = []
    for i, (start, landing, target) in enumerate(
        ((height, 0, below), (2, height + 2, above))
    ):
        copy = pltpu.make_async_remote_copy(
            src_ref=xs.at[:, pl.ds(start * c_in, 2 * c_in), :],
            dst_ref=xs.at[:, pl.ds(landing * c_in, 2 * c_in), :],
            send_sem=send_sem.at[n_chan - 1 + i],
            recv_sem=recv_sem.at[n_chan - 1 + i],
            device_id={"space": target},
            device_id_type=MESH,
        )
        copy.start()
        halos.append(copy)
    for h in range(2, height - 2):
        turn(h)
    xs[:, pl.ds((height + 4) * c_in, c_in), :] = jnp.zeros((2, c_in, width), BF)

    lanes = 4 * c_in

    def lay_filters(k):
        source = lax.rem(c + n_chan - k, n_chan)
        for e in range(3):
            for od in range(2):
                at = pl.ds(k * 6 * own + (e * 2 + od) * own, own)
                for i in range(2):
                    w1[at, pl.ds(i * lanes, lanes)] = gathered[source, e * 3 + i - od + 1]

    def layer_one(r, first_k, last_k):
        window = pl.ds(pl.multiple_of(r * c_in, c_in), lanes)
        stacked = jnp.concatenate([xs[0, window, :], xs[1, window, :]], axis=0)
        matrix = w1[first_k * 6 * own : last_k * 6 * own]
        product = jnp.dot(matrix, stacked, preferred_element_type=F32)
        for k in range(first_k, last_k):
            part = product[(k - first_k) * 6 * own : (k - first_k + 1) * 6 * own]
            row = jnp.maximum(combine_width(part, 2 * own), 0.0).astype(BF)
            source = lax.rem(c + n_chan - k, n_chan)
            for od in range(2):
                at = pl.multiple_of(r * 2 * c_mid + od * c_mid + source * own, own)
                hid[pl.ds(at, own), :] = row[od * own : (od + 1) * own]

    lay_filters(0)
    lax.fori_loop(2, height - 1, lambda r, _: layer_one(r, 0, 1), None, unroll=4)

    loads[2].wait()
    for e in range(3):
        for od in range(2):
            w2[pl.ds((e * 2 + od) * own, own), :] = jnp.concatenate(
                [second[i - od + 1, b, e] for b in range(3) for i in range(2)], axis=1
            )

    for copy in copies:
        copy.wait()
    for k in range(1, n_chan):
        lay_filters(k)
    lax.fori_loop(2, height - 1, lambda r, _: layer_one(r, 1, n_chan), None, unroll=2)
    for copy in halos:
        copy.wait()

    @pl.when(position == 0)
    def _():
        xs[:, : 2 * c_in, :] = jnp.zeros((2, 2 * c_in, width), BF)

    @pl.when(position == n_space - 1)
    def _():
        xs[:, pl.ds((height + 2) * c_in, 2 * c_in), :] = jnp.zeros((2, 2 * c_in, width), BF)

    lax.fori_loop(0, 2, lambda r, _: layer_one(r, 0, n_chan), None, unroll=1)
    lax.fori_loop(height - 1, height + 2, lambda r, _: layer_one(r, 0, n_chan), None, unroll=1)

    @pl.when(position == 0)
    def _():
        hid[: 2 * c_mid, :] = jnp.zeros((2 * c_mid, width), BF)

    @pl.when(position == n_space - 1)
    def _():
        hid[pl.ds((height + 1) * 2 * c_mid, 2 * c_mid), :] = jnp.zeros((2 * c_mid, width), BF)

    def layer_two(r):
        window = pl.ds(pl.multiple_of(r * 2 * c_mid, 2 * c_mid), 6 * c_mid)
        product = jnp.dot(w2[...], hid[window, :], preferred_element_type=F32)
        row = jnp.maximum(combine_width(product, 2 * own), 0.0)
        for d in range(2):
            for t in range(tiles):
                rows_out[d, t, pl.ds(pl.multiple_of(r * own, own), own), :] = row[
                    d * own : (d + 1) * own, t * LANES : (t + 1) * LANES
                ]

    lax.fori_loop(0, height, lambda r, _: layer_two(r), None, unroll=4)
    for d in range(2):
        for o in range(own):
            for t in range(tiles):
                out_ref[o, d, :, pl.ds(t * LANES, LANES)] = rows_out[
                    d, t, pl.ds(o, height, stride=own), :
                ].astype(BF)


def one_layer_of_tiles(voxels, first_filters, second_filters):
    n_space, n_chan = lax.axis_size("space"), lax.axis_size("chan")
    c_in, depth, height, width = voxels.shape
    own, c_mid = second_filters.shape[3:]
    sizes = (n_space, n_chan, c_in, own, c_mid, height, width)
    any_space = pl.BlockSpec(memory_space=pl.ANY)
    return pl.pallas_call(
        functools.partial(tile_kernel, sizes),
        out_shape=jax.ShapeDtypeStruct((own, depth, height, width), BF),
        in_specs=[any_space] * 3,
        out_specs=pl.BlockSpec(memory_space=pltpu.VMEM),
        scratch_shapes=[
            pltpu.VMEM(voxels.shape, BF),
            pltpu.VMEM(first_filters.shape, BF),
            pltpu.VMEM(second_filters.shape, BF),
            pltpu.VMEM((2, width // LANES, c_in * height, LANES), F32),
            pltpu.VMEM((2, (height + 5) * c_in, width), BF),
            pltpu.VMEM((n_chan, 9, own, 4 * c_in), BF),
            pltpu.VMEM((6 * c_mid, 8 * c_in), BF),
            pltpu.VMEM((6 * own, 6 * c_mid), BF),
            pltpu.VMEM(((height + 2) * 2 * c_mid, width), BF),
            pltpu.VMEM((2, width // LANES, height * own, LANES), F32),
            pltpu.SemaphoreType.DMA((3,)),
            pltpu.SemaphoreType.DMA((n_chan + 1,)),
            pltpu.SemaphoreType.DMA((n_chan + 1,)),
        ],
        compiler_params=pltpu.CompilerParams(
            collective_id=0, has_side_effects=True, vmem_limit_bytes=60 * 1024 * 1024
        ),
    )(voxels, first_filters, second_filters)


def solution(mesh):
    return jax.shard_map(
        one_layer_of_tiles if mesh.shape["space"] == GH else local,
        mesh=mesh,
        in_specs=(
            P(None, "space", None, None),
            P(None, None, None, "chan", None),
            P(None, None, None, "chan", None),
        ),
        out_specs=P("chan", "space", None, None),
        check_vma=False,
    )
```

```python
import functools

import jax
import jax.numpy as jnp
from jax import lax
from jax.experimental import pallas as pl
from jax.experimental.pallas import tpu as pltpu
from jax.sharding import PartitionSpec as P

GH = 8


def passed_along(value, axis, steps):
    count = lax.axis_size(axis)
    pairs = [(source, (source + steps) % count) for source in range(count)]
    return lax.ppermute(value, axis, pairs)


def extended(value, sides, width):
    for axis, dim in sides:
        size, length = (lax.axis_size(axis), value.shape[dim])
        up = [(i, (i + 1) % size) for i in range(size - 1)]
        down = [(j, i) for i, j in up]
        last = lax.slice_in_dim(value, length - width, length, axis=dim)
        initial = lax.slice_in_dim(value, 0, width, axis=dim)
        before = lax.ppermute(last, axis, up)
        after = lax.ppermute(initial, axis, down)
        value = jnp.concatenate([before, value, after], axis=dim)
    return value


def stack_taps(sided):
    return jnp.concatenate([sided[..., :-2], sided[..., 1:-1], sided[..., 2:]], 0)


def tile_border(volume_tile, above, below, front, back):
    tile_count = lax.axis_size("space")
    position = (lax.axis_index("space") + GH + GH // 4) % tile_count
    tile_row = position % GH
    depth_tile = position // GH
    grid_depth = tile_count // GH
    above_rim = above(volume_tile[:, :, -1:, :])
    below_rim = below(volume_tile[:, :, :1, :])
    above_rim = jnp.where(tile_row > 0, above_rim, jnp.zeros_like(above_rim))
    below_rim = jnp.where(tile_row < GH - 1, below_rim, jnp.zeros_like(below_rim))
    taller = jnp.concatenate([above_rim, volume_tile, below_rim], 2)
    front_rim = front(taller[:, -1:])
    back_rim = back(taller[:, :1])
    front_rim = jnp.where(depth_tile > 0, front_rim, jnp.zeros_like(front_rim))
    back_rim = jnp.where(depth_tile < grid_depth - 1, back_rim, jnp.zeros_like(back_rim))
    return jnp.concatenate([front_rim, taller, back_rim], 1)


def input_above(rim_cells):
    return passed_along(rim_cells, "space", 1)


def input_below(rim_cells):
    return passed_along(rim_cells, "space", -1)


def input_front(rim_cells):
    return passed_along(rim_cells, "space", GH)


def input_back(rim_cells):
    return passed_along(rim_cells, "space", -GH)


def hidden_above(rim_cells):
    return passed_along(rim_cells, "space", 1)


def hidden_below(rim_cells):
    return passed_along(rim_cells, "space", -1)


def hidden_front(rim_cells):
    return passed_along(rim_cells, "space", GH)


def hidden_back(rim_cells):
    return passed_along(rim_cells, "space", -GH)


def correlate(stacked, filters, depth_rows, height_rows):
    out_count = filters.shape[3]
    running = jnp.zeros((out_count, depth_rows, height_rows, stacked.shape[3]), jnp.float32)
    for depth_tap in range(3):
        for height_tap in range(3):
            matrix = filters[depth_tap, height_tap].transpose(1, 0, 2).reshape(out_count, -1)
            window = stacked[
                :, depth_tap : depth_tap + depth_rows, height_tap : height_tap + height_rows, :
            ]
            running = running + jnp.einsum(
                "ok,kdhw->odhw", matrix, window, preferred_element_type=jnp.float32
            )
    return running


def local(voxels, first_filters, second_filters):
    depth_rows = voxels.shape[1]
    height_rows = voxels.shape[2]
    width_cells = voxels.shape[3]
    share = width_cells // lax.axis_size("chan")
    own_cols = lax.dynamic_slice_in_dim(voxels, lax.axis_index("chan") * share, share, 3)
    every_first, every_second = (
        lax.all_gather(first_filters, "chan", axis=3, tiled=True),
        lax.all_gather(second_filters, "chan", axis=3, tiled=True),
    )
    sided = extended(own_cols, (("chan", 3),), 1)
    padded = tile_border(sided, input_above, input_below, input_front, input_back)
    hidden = jax.nn.relu(
        correlate(stack_taps(padded), every_first, depth_rows, height_rows)
    ).astype(jnp.bfloat16)
    hidden_sided = extended(hidden, (("chan", 3),), 1)
    hidden_pad = tile_border(hidden_sided, hidden_above, hidden_below, hidden_front, hidden_back)
    result = jax.nn.relu(
        correlate(stack_taps(hidden_pad), every_second, depth_rows, height_rows)
    ).astype(jnp.bfloat16)
    return lax.all_to_all(result, "chan", split_axis=0, concat_axis=3, tiled=True)


MESH = pl.DeviceIdType.MESH
BF = jnp.bfloat16
F32 = jnp.float32
LANES = 128


def combine_width(product, part):
    lane = lax.broadcasted_iota(jnp.int32, (part, product.shape[1]), 1)
    width = product.shape[1]
    left = jnp.where(lane == 0, 0.0, pltpu.roll(product[:part], 1, 1))
    right = jnp.where(lane == width - 1, 0.0, pltpu.roll(product[2 * part :], width - 1, 1))
    return left + product[part : 2 * part] + right


def tile_kernel(
    sizes, vox_hbm, first_hbm, second_hbm, out_ref,
    vox, first, second, wide, xs, gathered, w1, w2, hid, rows_out,
    load_sem, send_sem, recv_sem,
):
    n_space, n_chan, c_in, own, c_mid, height, width = sizes
    s = lax.axis_index("space")
    c = lax.axis_index("chan")
    below, above = lax.rem(s + 1, n_space), lax.rem(s + n_space - 1, n_space)
    position = lax.rem(s + GH + GH // 4, n_space)

    loads = [
        pltpu.make_async_copy(first_hbm, first, load_sem.at[0]),
        pltpu.make_async_copy(vox_hbm, vox, load_sem.at[1]),
        pltpu.make_async_copy(second_hbm, second, load_sem.at[2]),
    ]
    for load in loads:
        load.start()

    barrier = pltpu.get_barrier_semaphore()
    for neighbour in (below, above):
        pl.semaphore_signal(barrier, inc=1, device_id={"space": neighbour}, device_id_type=MESH)
    for k in range(1, n_chan):
        pl.semaphore_signal(
            barrier, inc=1, device_id={"chan": lax.rem(c + k, n_chan)}, device_id_type=MESH
        )

    loads[0].wait()
    spare = jnp.zeros((own, c_in), BF)
    for e in range(3):
        for a in range(3):
            gathered[c, e * 3 + a] = jnp.concatenate(
                [first[a, 0, e], first[a, 1, e], first[a, 2, e], spare], axis=1
            )
    loads[1].wait()
    tiles = width // LANES
    for d in range(2):
        for t in range(tiles):
            part = vox[:, d, :, pl.ds(t * LANES, LANES)].astype(F32)
            wide[d, t] = part.reshape(c_in * height, LANES)

    def turn(h):
        for d in range(2):
            for t in range(tiles):
                xs[d, pl.ds((h + 2) * c_in, c_in), pl.ds(t * LANES, LANES)] = wide[
                    d, t, pl.ds(h, c_in, stride=height), :
                ].astype(BF)

    for h in (0, 1, height - 2, height - 1):
        turn(h)

    pl.semaphore_wait(barrier, n_chan + 1)
    copies = []
    for k in range(1, n_chan):
        copy = pltpu.make_async_remote_copy(
            src_ref=gathered.at[c],
            dst_ref=gathered.at[c],
            send_sem=send_sem.at[k - 1],
            recv_sem=recv_sem.at[k - 1],
            device_id={"chan": lax.rem(c + k, n_chan)},
            device_id_type=MESH,
        )
        copy.start()
        copies.append(copy)
    halos = []
    for i, (start, landing, target) in enumerate(
        ((height, 0, below), (2, height + 2, above))
    ):
        copy = pltpu.make_async_remote_copy(
            src_ref=xs.at[:, pl.ds(start * c_in, 2 * c_in), :],
            dst_ref=xs.at[:, pl.ds(landing * c_in, 2 * c_in), :],
            send_sem=send_sem.at[n_chan - 1 + i],
            recv_sem=recv_sem.at[n_chan - 1 + i],
            device_id={"space": target},
            device_id_type=MESH,
        )
        copy.start()
        halos.append(copy)
    for h in range(2, height - 2):
        turn(h)
    xs[:, pl.ds((height + 4) * c_in, c_in), :] = jnp.zeros((2, c_in, width), BF)

    lanes = 4 * c_in

    def lay_filters(k):
        source = lax.rem(c + n_chan - k, n_chan)
        for e in range(3):
            for od in range(2):
                at = pl.ds(k * 6 * own + (e * 2 + od) * own, own)
                for i in range(2):
                    w1[at, pl.ds(i * lanes, lanes)] = gathered[source, e * 3 + i - od + 1]

    def layer_one(r, first_k, last_k):
        window = pl.ds(pl.multiple_of(r * c_in, c_in), lanes)
        stacked = jnp.concatenate([xs[0, window, :], xs[1, window, :]], axis=0)
        matrix = w1[first_k * 6 * own : last_k * 6 * own]
        product = jnp.dot(matrix, stacked, preferred_element_type=F32)
        for k in range(first_k, last_k):
            part = product[(k - first_k) * 6 * own : (k - first_k + 1) * 6 * own]
            row = jnp.maximum(combine_width(part, 2 * own), 0.0).astype(BF)
            source = lax.rem(c + n_chan - k, n_chan)
            for od in range(2):
                at = pl.multiple_of(r * 2 * c_mid + od * c_mid + source * own, own)
                hid[pl.ds(at, own), :] = row[od * own : (od + 1) * own]

    lay_filters(0)
    lax.fori_loop(2, height - 1, lambda r, _: layer_one(r, 0, 1), None, unroll=13)

    loads[2].wait()
    for e in range(3):
        for od in range(2):
            w2[pl.ds((e * 2 + od) * own, own), :] = jnp.concatenate(
                [second[i - od + 1, b, e] for b in range(3) for i in range(2)], axis=1
            )

    for copy in copies:
        copy.wait()
    for k in range(1, n_chan):
        lay_filters(k)
    lax.fori_loop(2, height - 1, lambda r, _: layer_one(r, 1, n_chan), None, unroll=13)
    for copy in halos:
        copy.wait()

    @pl.when(position == 0)
    def _():
        xs[:, : 2 * c_in, :] = jnp.zeros((2, 2 * c_in, width), BF)

    @pl.when(position == n_space - 1)
    def _():
        xs[:, pl.ds((height + 2) * c_in, 2 * c_in), :] = jnp.zeros((2, 2 * c_in, width), BF)

    lax.fori_loop(0, 2, lambda r, _: layer_one(r, 0, n_chan), None, unroll=3)
    lax.fori_loop(height - 1, height + 2, lambda r, _: layer_one(r, 0, n_chan), None, unroll=3)

    @pl.when(position == 0)
    def _():
        hid[: 2 * c_mid, :] = jnp.zeros((2 * c_mid, width), BF)

    @pl.when(position == n_space - 1)
    def _():
        hid[pl.ds((height + 1) * 2 * c_mid, 2 * c_mid), :] = jnp.zeros((2 * c_mid, width), BF)

    def layer_two(r):
        window = pl.ds(pl.multiple_of(r * 2 * c_mid, 2 * c_mid), 6 * c_mid)
        product = jnp.dot(w2[...], hid[window, :], preferred_element_type=F32)
        row = jnp.maximum(combine_width(product, 2 * own), 0.0)
        for d in range(2):
            for t in range(tiles):
                rows_out[d, t, pl.ds(pl.multiple_of(r * own, own), own), :] = row[
                    d * own : (d + 1) * own, t * LANES : (t + 1) * LANES
                ]

    lax.fori_loop(0, height, lambda r, _: layer_two(r), None, unroll=16)
    for d in range(2):
        for o in range(own):
            for t in range(tiles):
                out_ref[o, d, :, pl.ds(t * LANES, LANES)] = rows_out[
                    d, t, pl.ds(o, height, stride=own), :
                ].astype(BF)


def one_layer_of_tiles(voxels, first_filters, second_filters):
    n_space, n_chan = lax.axis_size("space"), lax.axis_size("chan")
    c_in, depth, height, width = voxels.shape
    own, c_mid = second_filters.shape[3:]
    sizes = (n_space, n_chan, c_in, own, c_mid, height, width)
    any_space = pl.BlockSpec(memory_space=pl.ANY)
    return pl.pallas_call(
        functools.partial(tile_kernel, sizes),
        out_shape=jax.ShapeDtypeStruct((own, depth, height, width), BF),
        in_specs=[any_space] * 3,
        out_specs=pl.BlockSpec(memory_space=pltpu.VMEM),
        scratch_shapes=[
            pltpu.VMEM(voxels.shape, BF),
            pltpu.VMEM(first_filters.shape, BF),
            pltpu.VMEM(second_filters.shape, BF),
            pltpu.VMEM((2, width // LANES, c_in * height, LANES), F32),
            pltpu.VMEM((2, (height + 5) * c_in, width), BF),
            pltpu.VMEM((n_chan, 9, own, 4 * c_in), BF),
            pltpu.VMEM((6 * c_mid, 8 * c_in), BF),
            pltpu.VMEM((6 * own, 6 * c_mid), BF),
            pltpu.VMEM(((height + 2) * 2 * c_mid, width), BF),
            pltpu.VMEM((2, width // LANES, height * own, LANES), F32),
            pltpu.SemaphoreType.DMA((3,)),
            pltpu.SemaphoreType.DMA((n_chan + 1,)),
            pltpu.SemaphoreType.DMA((n_chan + 1,)),
        ],
        compiler_params=pltpu.CompilerParams(
            collective_id=0, has_side_effects=True, vmem_limit_bytes=60 * 1024 * 1024
        ),
    )(voxels, first_filters, second_filters)


def solution(mesh):
    return jax.shard_map(
        one_layer_of_tiles if mesh.shape["space"] == GH else local,
        mesh=mesh,
        in_specs=(
            P(None, "space", None, None),
            P(None, None, None, "chan", None),
            P(None, None, None, "chan", None),
        ),
        out_specs=P("chan", "space", None, None),
        check_vma=False,
    )
```

```python
import functools

import jax
import jax.numpy as jnp
from jax import lax
from jax.experimental import pallas as pl
from jax.experimental.pallas import tpu as pltpu
from jax.sharding import PartitionSpec as P

GH = 8


def passed_along(value, axis, steps):
    count = lax.axis_size(axis)
    pairs = [(source, (source + steps) % count) for source in range(count)]
    return lax.ppermute(value, axis, pairs)


def extended(value, sides, width):
    for axis, dim in sides:
        size, length = (lax.axis_size(axis), value.shape[dim])
        up = [(i, (i + 1) % size) for i in range(size - 1)]
        down = [(j, i) for i, j in up]
        last = lax.slice_in_dim(value, length - width, length, axis=dim)
        initial = lax.slice_in_dim(value, 0, width, axis=dim)
        before = lax.ppermute(last, axis, up)
        after = lax.ppermute(initial, axis, down)
        value = jnp.concatenate([before, value, after], axis=dim)
    return value


def stack_taps(sided):
    return jnp.concatenate([sided[..., :-2], sided[..., 1:-1], sided[..., 2:]], 0)


def tile_border(volume_tile, above, below, front, back):
    tile_count = lax.axis_size("space")
    position = (lax.axis_index("space") + GH + GH // 4) % tile_count
    tile_row = position % GH
    depth_tile = position // GH
    grid_depth = tile_count // GH
    above_rim = above(volume_tile[:, :, -1:, :])
    below_rim = below(volume_tile[:, :, :1, :])
    above_rim = jnp.where(tile_row > 0, above_rim, jnp.zeros_like(above_rim))
    below_rim = jnp.where(tile_row < GH - 1, below_rim, jnp.zeros_like(below_rim))
    taller = jnp.concatenate([above_rim, volume_tile, below_rim], 2)
    front_rim = front(taller[:, -1:])
    back_rim = back(taller[:, :1])
    front_rim = jnp.where(depth_tile > 0, front_rim, jnp.zeros_like(front_rim))
    back_rim = jnp.where(depth_tile < grid_depth - 1, back_rim, jnp.zeros_like(back_rim))
    return jnp.concatenate([front_rim, taller, back_rim], 1)


def input_above(rim_cells):
    return passed_along(rim_cells, "space", 1)


def input_below(rim_cells):
    return passed_along(rim_cells, "space", -1)


def input_front(rim_cells):
    return passed_along(rim_cells, "space", GH)


def input_back(rim_cells):
    return passed_along(rim_cells, "space", -GH)


def hidden_above(rim_cells):
    return passed_along(rim_cells, "space", 1)


def hidden_below(rim_cells):
    return passed_along(rim_cells, "space", -1)


def hidden_front(rim_cells):
    return passed_along(rim_cells, "space", GH)


def hidden_back(rim_cells):
    return passed_along(rim_cells, "space", -GH)


def correlate(stacked, filters, depth_rows, height_rows):
    out_count = filters.shape[3]
    running = jnp.zeros((out_count, depth_rows, height_rows, stacked.shape[3]), jnp.float32)
    for depth_tap in range(3):
        for height_tap in range(3):
            matrix = filters[depth_tap, height_tap].transpose(1, 0, 2).reshape(out_count, -1)
            window = stacked[
                :, depth_tap : depth_tap + depth_rows, height_tap : height_tap + height_rows, :
            ]
            running = running + jnp.einsum(
                "ok,kdhw->odhw", matrix, window, preferred_element_type=jnp.float32
            )
    return running


def local(voxels, first_filters, second_filters):
    depth_rows = voxels.shape[1]
    height_rows = voxels.shape[2]
    width_cells = voxels.shape[3]
    share = width_cells // lax.axis_size("chan")
    own_cols = lax.dynamic_slice_in_dim(voxels, lax.axis_index("chan") * share, share, 3)
    every_first, every_second = (
        lax.all_gather(first_filters, "chan", axis=3, tiled=True),
        lax.all_gather(second_filters, "chan", axis=3, tiled=True),
    )
    sided = extended(own_cols, (("chan", 3),), 1)
    padded = tile_border(sided, input_above, input_below, input_front, input_back)
    hidden = jax.nn.relu(
        correlate(stack_taps(padded), every_first, depth_rows, height_rows)
    ).astype(jnp.bfloat16)
    hidden_sided = extended(hidden, (("chan", 3),), 1)
    hidden_pad = tile_border(hidden_sided, hidden_above, hidden_below, hidden_front, hidden_back)
    result = jax.nn.relu(
        correlate(stack_taps(hidden_pad), every_second, depth_rows, height_rows)
    ).astype(jnp.bfloat16)
    return lax.all_to_all(result, "chan", split_axis=0, concat_axis=3, tiled=True)


MESH = pl.DeviceIdType.MESH
BF = jnp.bfloat16
F32 = jnp.float32
LANES = 128


def combine_width(product, part):
    lane = lax.broadcasted_iota(jnp.int32, (part, product.shape[1]), 1)
    width = product.shape[1]
    left = jnp.where(lane == 0, 0.0, pltpu.roll(product[:part], 1, 1))
    right = jnp.where(lane == width - 1, 0.0, pltpu.roll(product[2 * part :], width - 1, 1))
    return left + product[part : 2 * part] + right


def tile_kernel(
    sizes, vox_hbm, first_hbm, second_hbm, out_ref,
    vox, first, second, wide, xs, gathered, w1, w2, hid, rows_out,
    load_sem, send_sem, recv_sem,
):
    n_space, n_chan, c_in, own, c_mid, height, width = sizes
    s = lax.axis_index("space")
    c = lax.axis_index("chan")
    below, above = lax.rem(s + 1, n_space), lax.rem(s + n_space - 1, n_space)
    position = lax.rem(s + GH + GH // 4, n_space)

    loads = [
        pltpu.make_async_copy(first_hbm, first, load_sem.at[0]),
        pltpu.make_async_copy(vox_hbm, vox, load_sem.at[1]),
        pltpu.make_async_copy(second_hbm, second, load_sem.at[2]),
    ]
    for load in loads:
        load.start()

    barrier = pltpu.get_barrier_semaphore()
    for neighbour in (below, above):
        pl.semaphore_signal(barrier, inc=1, device_id={"space": neighbour}, device_id_type=MESH)
    for k in range(1, n_chan):
        pl.semaphore_signal(
            barrier, inc=1, device_id={"chan": lax.rem(c + k, n_chan)}, device_id_type=MESH
        )

    loads[0].wait()
    spare = jnp.zeros((own, c_in), BF)
    pieces = [first[a, b, e] for e in range(3) for a in range(3) for b in range(3)]
    gathered[c] = jnp.concatenate(pieces + [spare] * (-len(pieces) % (LANES // c_in)), axis=1)

    loads[1].wait()
    tiles = width // LANES
    for d in range(2):
        for t in range(tiles):
            part = vox[:, d, :, pl.ds(t * LANES, LANES)].astype(F32)
            wide[d, t] = part.reshape(c_in * height, LANES)

    def turn(h):
        for d in range(2):
            for t in range(tiles):
                xs[d, pl.ds((h + 2) * c_in, c_in), pl.ds(t * LANES, LANES)] = wide[
                    d, t, pl.ds(h, c_in, stride=height), :
                ].astype(BF)

    for h in (0, 1, height - 2, height - 1):
        turn(h)

    pl.semaphore_wait(barrier, n_chan + 1)
    copies = []
    for k in range(1, n_chan):
        copy = pltpu.make_async_remote_copy(
            src_ref=gathered.at[c],
            dst_ref=gathered.at[c],
            send_sem=send_sem.at[k - 1],
            recv_sem=recv_sem.at[k - 1],
            device_id={"chan": lax.rem(c + k, n_chan)},
            device_id_type=MESH,
        )
        copy.start()
        copies.append(copy)
    halos = []
    for i, (start, landing, target) in enumerate(
        ((height, 0, below), (2, height + 2, above))
    ):
        copy = pltpu.make_async_remote_copy(
            src_ref=xs.at[:, pl.ds(start * c_in, 2 * c_in), :],
            dst_ref=xs.at[:, pl.ds(landing * c_in, 2 * c_in), :],
            send_sem=send_sem.at[n_chan - 1 + i],
            recv_sem=recv_sem.at[n_chan - 1 + i],
            device_id={"space": target},
            device_id_type=MESH,
        )
        copy.start()
        halos.append(copy)
    for h in range(2, height - 2):
        turn(h)
    xs[:, pl.ds((height + 4) * c_in, c_in), :] = jnp.zeros((2, c_in, width), BF)

    lanes = 4 * c_in

    def lay_filters(k):
        source = lax.rem(c + n_chan - k, n_chan)
        whole = gathered[source]
        for e in range(3):
            for od in range(2):
                at = pl.ds(k * 6 * own + (e * 2 + od) * own, own)
                for i in range(2):
                    start = (e * 3 + i - od + 1) * 3 * c_in
                    taps = whole[:, start : start + 3 * c_in]
                    w1[at, pl.ds(i * lanes, lanes)] = jnp.concatenate([taps, spare], axis=1)

    def layer_one(r, first_k, last_k):
        window = pl.ds(pl.multiple_of(r * c_in, c_in), lanes)
        stacked = jnp.concatenate([xs[0, window, :], xs[1, window, :]], axis=0)
        matrix = w1[first_k * 6 * own : last_k * 6 * own]
        product = jnp.dot(matrix, stacked, preferred_element_type=F32)
        for k in range(first_k, last_k):
            part = product[(k - first_k) * 6 * own : (k - first_k + 1) * 6 * own]
            row = jnp.maximum(combine_width(part, 2 * own), 0.0).astype(BF)
            source = lax.rem(c + n_chan - k, n_chan)
            for od in range(2):
                at = pl.multiple_of(r * 2 * c_mid + od * c_mid + source * own, own)
                hid[pl.ds(at, own), :] = row[od * own : (od + 1) * own]

    lay_filters(0)
    lax.fori_loop(2, height - 1, lambda r, _: layer_one(r, 0, 1), None, unroll=13)

    loads[2].wait()
    for e in range(3):
        for od in range(2):
            w2[pl.ds((e * 2 + od) * own, own), :] = jnp.concatenate(
                [second[i - od + 1, b, e] for b in range(3) for i in range(2)], axis=1
            )

    for copy in copies:
        copy.wait()
    for k in range(1, n_chan):
        lay_filters(k)
    lax.fori_loop(2, height - 1, lambda r, _: layer_one(r, 1, n_chan), None, unroll=13)
    for copy in halos:
        copy.wait()

    for edge, start in ((0, 0), (n_space - 1, height + 2)):
        at = pl.ds(start * c_in, 2 * c_in)
        xs[:, at, :] = jnp.where(position == edge, jnp.zeros((), BF), xs[:, at, :])
    lax.fori_loop(0, 2, lambda r, _: layer_one(r, 0, n_chan), None, unroll=3)
    lax.fori_loop(height - 1, height + 2, lambda r, _: layer_one(r, 0, n_chan), None, unroll=3)

    for edge, start in ((0, 0), (n_space - 1, height + 1)):
        at = pl.ds(start * 2 * c_mid, 2 * c_mid)
        hid[at, :] = jnp.where(position == edge, jnp.zeros((), BF), hid[at, :])

    def layer_two(r):
        window = pl.ds(pl.multiple_of(r * 2 * c_mid, 2 * c_mid), 6 * c_mid)
        product = jnp.dot(w2[...], hid[window, :], preferred_element_type=F32)
        row = jnp.maximum(combine_width(product, 2 * own), 0.0)
        for d in range(2):
            for t in range(tiles):
                rows_out[d, t, pl.ds(pl.multiple_of(r * own, own), own), :] = row[
                    d * own : (d + 1) * own, t * LANES : (t + 1) * LANES
                ]

    lax.fori_loop(0, height, lambda r, _: layer_two(r), None, unroll=16)
    for d in range(2):
        for o in range(own):
            for t in range(tiles):
                out_ref[o, d, :, pl.ds(t * LANES, LANES)] = rows_out[
                    d, t, pl.ds(o, height, stride=own), :
                ].astype(BF)


def one_layer_of_tiles(voxels, first_filters, second_filters):
    n_space, n_chan = lax.axis_size("space"), lax.axis_size("chan")
    c_in, depth, height, width = voxels.shape
    own, c_mid = second_filters.shape[3:]
    sizes = (n_space, n_chan, c_in, own, c_mid, height, width)
    any_space = pl.BlockSpec(memory_space=pl.ANY)
    return pl.pallas_call(
        functools.partial(tile_kernel, sizes),
        out_shape=jax.ShapeDtypeStruct((own, depth, height, width), BF),
        in_specs=[any_space] * 3,
        out_specs=pl.BlockSpec(memory_space=pltpu.VMEM),
        scratch_shapes=[
            pltpu.VMEM(voxels.shape, BF),
            pltpu.VMEM(first_filters.shape, BF),
            pltpu.VMEM(second_filters.shape, BF),
            pltpu.VMEM((2, width // LANES, c_in * height, LANES), F32),
            pltpu.VMEM((2, (height + 5) * c_in, width), BF),
            pltpu.VMEM((n_chan, own, pl.cdiv(27 * c_in, LANES) * LANES), BF),
            pltpu.VMEM((6 * c_mid, 8 * c_in), BF),
            pltpu.VMEM((6 * own, 6 * c_mid), BF),
            pltpu.VMEM(((height + 2) * 2 * c_mid, width), BF),
            pltpu.VMEM((2, width // LANES, height * own, LANES), F32),
            pltpu.SemaphoreType.DMA((3,)),
            pltpu.SemaphoreType.DMA((n_chan + 1,)),
            pltpu.SemaphoreType.DMA((n_chan + 1,)),
        ],
        compiler_params=pltpu.CompilerParams(
            collective_id=0, has_side_effects=True, vmem_limit_bytes=60 * 1024 * 1024
        ),
    )(voxels, first_filters, second_filters)


def solution(mesh):
    return jax.shard_map(
        one_layer_of_tiles if mesh.shape["space"] == GH else local,
        mesh=mesh,
        in_specs=(
            P(None, "space", None, None),
            P(None, None, None, "chan", None),
            P(None, None, None, "chan", None),
        ),
        out_specs=P("chan", "space", None, None),
        check_vma=False,
    )
```

```python
import functools

import jax
import jax.numpy as jnp
from jax import lax
from jax.experimental import pallas as pl
from jax.experimental.pallas import tpu as pltpu
from jax.sharding import PartitionSpec as P

GH = 8


def passed_along(value, axis, steps):
    count = lax.axis_size(axis)
    pairs = [(source, (source + steps) % count) for source in range(count)]
    return lax.ppermute(value, axis, pairs)


def extended(value, sides, width):
    for axis, dim in sides:
        size, length = (lax.axis_size(axis), value.shape[dim])
        up = [(i, (i + 1) % size) for i in range(size - 1)]
        down = [(j, i) for i, j in up]
        last = lax.slice_in_dim(value, length - width, length, axis=dim)
        initial = lax.slice_in_dim(value, 0, width, axis=dim)
        before = lax.ppermute(last, axis, up)
        after = lax.ppermute(initial, axis, down)
        value = jnp.concatenate([before, value, after], axis=dim)
    return value


def stack_taps(sided):
    return jnp.concatenate([sided[..., :-2], sided[..., 1:-1], sided[..., 2:]], 0)


def tile_border(volume_tile, above, below, front, back):
    tile_count = lax.axis_size("space")
    position = (lax.axis_index("space") + GH + GH // 4) % tile_count
    tile_row = position % GH
    depth_tile = position // GH
    grid_depth = tile_count // GH
    above_rim = above(volume_tile[:, :, -1:, :])
    below_rim = below(volume_tile[:, :, :1, :])
    above_rim = jnp.where(tile_row > 0, above_rim, jnp.zeros_like(above_rim))
    below_rim = jnp.where(tile_row < GH - 1, below_rim, jnp.zeros_like(below_rim))
    taller = jnp.concatenate([above_rim, volume_tile, below_rim], 2)
    front_rim = front(taller[:, -1:])
    back_rim = back(taller[:, :1])
    front_rim = jnp.where(depth_tile > 0, front_rim, jnp.zeros_like(front_rim))
    back_rim = jnp.where(depth_tile < grid_depth - 1, back_rim, jnp.zeros_like(back_rim))
    return jnp.concatenate([front_rim, taller, back_rim], 1)


def input_above(rim_cells):
    return passed_along(rim_cells, "space", 1)


def input_below(rim_cells):
    return passed_along(rim_cells, "space", -1)


def input_front(rim_cells):
    return passed_along(rim_cells, "space", GH)


def input_back(rim_cells):
    return passed_along(rim_cells, "space", -GH)


def hidden_above(rim_cells):
    return passed_along(rim_cells, "space", 1)


def hidden_below(rim_cells):
    return passed_along(rim_cells, "space", -1)


def hidden_front(rim_cells):
    return passed_along(rim_cells, "space", GH)


def hidden_back(rim_cells):
    return passed_along(rim_cells, "space", -GH)


def correlate(stacked, filters, depth_rows, height_rows):
    out_count = filters.shape[3]
    running = jnp.zeros((out_count, depth_rows, height_rows, stacked.shape[3]), jnp.float32)
    for depth_tap in range(3):
        for height_tap in range(3):
            matrix = filters[depth_tap, height_tap].transpose(1, 0, 2).reshape(out_count, -1)
            window = stacked[
                :, depth_tap : depth_tap + depth_rows, height_tap : height_tap + height_rows, :
            ]
            running = running + jnp.einsum(
                "ok,kdhw->odhw", matrix, window, preferred_element_type=jnp.float32
            )
    return running


def local(voxels, first_filters, second_filters):
    depth_rows = voxels.shape[1]
    height_rows = voxels.shape[2]
    width_cells = voxels.shape[3]
    share = width_cells // lax.axis_size("chan")
    own_cols = lax.dynamic_slice_in_dim(voxels, lax.axis_index("chan") * share, share, 3)
    every_first, every_second = (
        lax.all_gather(first_filters, "chan", axis=3, tiled=True),
        lax.all_gather(second_filters, "chan", axis=3, tiled=True),
    )
    sided = extended(own_cols, (("chan", 3),), 1)
    padded = tile_border(sided, input_above, input_below, input_front, input_back)
    hidden = jax.nn.relu(
        correlate(stack_taps(padded), every_first, depth_rows, height_rows)
    ).astype(jnp.bfloat16)
    hidden_sided = extended(hidden, (("chan", 3),), 1)
    hidden_pad = tile_border(hidden_sided, hidden_above, hidden_below, hidden_front, hidden_back)
    result = jax.nn.relu(
        correlate(stack_taps(hidden_pad), every_second, depth_rows, height_rows)
    ).astype(jnp.bfloat16)
    return lax.all_to_all(result, "chan", split_axis=0, concat_axis=3, tiled=True)


MESH = pl.DeviceIdType.MESH
BF = jnp.bfloat16
F32 = jnp.float32
LANES = 128


def combine_width(product, part):
    lane = lax.broadcasted_iota(jnp.int32, (part, product.shape[1]), 1)
    width = product.shape[1]
    left = jnp.where(lane == 0, 0.0, pltpu.roll(product[:part], 1, 1))
    right = jnp.where(lane == width - 1, 0.0, pltpu.roll(product[2 * part :], width - 1, 1))
    return left + product[part : 2 * part] + right


def tile_kernel(
    sizes, vox_hbm, first_hbm, second_hbm, out_ref,
    vox, first, second, wide, xs, gathered, w1, w2, hid, rows_out,
    load_sem, send_sem, recv_sem,
):
    n_space, n_chan, c_in, own, c_mid, height, width = sizes
    s = lax.axis_index("space")
    c = lax.axis_index("chan")
    below, above = lax.rem(s + 1, n_space), lax.rem(s + n_space - 1, n_space)
    position = lax.rem(s + GH + GH // 4, n_space)

    loads = [
        pltpu.make_async_copy(first_hbm, first, load_sem.at[0]),
        pltpu.make_async_copy(vox_hbm, vox, load_sem.at[1]),
        pltpu.make_async_copy(second_hbm, second, load_sem.at[2]),
    ]
    for load in loads:
        load.start()

    barrier = pltpu.get_barrier_semaphore()
    for neighbour in (below, above):
        pl.semaphore_signal(barrier, inc=1, device_id={"space": neighbour}, device_id_type=MESH)
    for k in range(1, n_chan):
        pl.semaphore_signal(
            barrier, inc=1, device_id={"chan": lax.rem(c + k, n_chan)}, device_id_type=MESH
        )

    loads[0].wait()
    spare = jnp.zeros((own, c_in), BF)
    pieces = [first[a, b, e] for e in range(3) for a in range(3) for b in range(3)]
    gathered[c] = jnp.concatenate(pieces + [spare] * (-len(pieces) % (LANES // c_in)), axis=1)

    loads[1].wait()
    tiles = width // LANES
    for d in range(2):
        for t in range(tiles):
            part = vox[:, d, :, pl.ds(t * LANES, LANES)].astype(F32)
            wide[d, t] = part.reshape(c_in * height, LANES)

    def turn(h):
        for d in range(2):
            for t in range(tiles):
                xs[d, pl.ds((h + 2) * c_in, c_in), pl.ds(t * LANES, LANES)] = wide[
                    d, t, pl.ds(h, c_in, stride=height), :
                ].astype(BF)

    for h in (0, 1, height - 2, height - 1):
        turn(h)

    pl.semaphore_wait(barrier, n_chan + 1)
    copies = []
    for k in range(1, n_chan):
        copy = pltpu.make_async_remote_copy(
            src_ref=gathered.at[c],
            dst_ref=gathered.at[c],
            send_sem=send_sem.at[k - 1],
            recv_sem=recv_sem.at[k - 1],
            device_id={"chan": lax.rem(c + k, n_chan)},
            device_id_type=MESH,
        )
        copy.start()
        copies.append(copy)
    halos = []
    for i, (start, landing, target) in enumerate(
        ((height, 0, below), (2, height + 2, above))
    ):
        copy = pltpu.make_async_remote_copy(
            src_ref=xs.at[:, pl.ds(start * c_in, 2 * c_in), :],
            dst_ref=xs.at[:, pl.ds(landing * c_in, 2 * c_in), :],
            send_sem=send_sem.at[n_chan - 1 + i],
            recv_sem=recv_sem.at[n_chan - 1 + i],
            device_id={"space": target},
            device_id_type=MESH,
        )
        copy.start()
        halos.append(copy)
    for h in range(2, height - 2):
        turn(h)
    xs[:, pl.ds((height + 4) * c_in, c_in), :] = jnp.zeros((2, c_in, width), BF)

    lanes = 4 * c_in

    def lay_filters(k):
        source = lax.rem(c + n_chan - k, n_chan)
        whole = gathered[source]
        for e in range(3):
            for od in range(2):
                at = pl.ds(k * 6 * own + (e * 2 + od) * own, own)
                for i in range(2):
                    start = (e * 3 + i - od + 1) * 3 * c_in
                    taps = whole[:, start : start + 3 * c_in]
                    w1[at, pl.ds(i * lanes, lanes)] = jnp.concatenate([taps, spare], axis=1)

    def layer_one(r, first_k, last_k):
        window = pl.ds(pl.multiple_of(r * c_in, c_in), lanes)
        stacked = jnp.concatenate([xs[0, window, :], xs[1, window, :]], axis=0)
        matrix = w1[first_k * 6 * own : last_k * 6 * own]
        product = jnp.dot(matrix, stacked, preferred_element_type=F32)
        for k in range(first_k, last_k):
            part = product[(k - first_k) * 6 * own : (k - first_k + 1) * 6 * own]
            row = jnp.maximum(combine_width(part, 2 * own), 0.0).astype(BF)
            source = lax.rem(c + n_chan - k, n_chan)
            for od in range(2):
                at = pl.multiple_of(r * 2 * c_mid + od * c_mid + source * own, own)
                hid[pl.ds(at, own), :] = row[od * own : (od + 1) * own]

    lay_filters(0)
    lax.fori_loop(2, height - 1, lambda r, _: layer_one(r, 0, 1), None, unroll=13)

    loads[2].wait()
    for e in range(3):
        for od in range(2):
            w2[pl.ds((e * 2 + od) * own, own), :] = jnp.concatenate(
                [second[i - od + 1, b, e] for b in range(3) for i in range(2)], axis=1
            )

    for copy in copies:
        copy.wait()
    for k in range(1, n_chan):
        lay_filters(k)
    lax.fori_loop(2, height - 1, lambda r, _: layer_one(r, 1, n_chan), None, unroll=13)
    def layer_two(r):
        window = pl.ds(pl.multiple_of(r * 2 * c_mid, 2 * c_mid), 6 * c_mid)
        product = jnp.dot(w2[...], hid[window, :], preferred_element_type=F32)
        row = jnp.maximum(combine_width(product, 2 * own), 0.0)
        for d in range(2):
            for t in range(tiles):
                rows_out[d, t, pl.ds(pl.multiple_of(r * own, own), own), :] = row[
                    d * own : (d + 1) * own, t * LANES : (t + 1) * LANES
                ]

    lax.fori_loop(2, height - 3, lambda r, _: layer_two(r), None, unroll=11)
    for copy in halos:
        copy.wait()

    for edge, start in ((0, 0), (n_space - 1, height + 2)):
        at = pl.ds(start * c_in, 2 * c_in)
        xs[:, at, :] = jnp.where(position == edge, jnp.zeros((), BF), xs[:, at, :])
    lax.fori_loop(0, 2, lambda r, _: layer_one(r, 0, n_chan), None, unroll=3)
    lax.fori_loop(height - 1, height + 2, lambda r, _: layer_one(r, 0, n_chan), None, unroll=3)

    for edge, start in ((0, 0), (n_space - 1, height + 1)):
        at = pl.ds(start * 2 * c_mid, 2 * c_mid)
        hid[at, :] = jnp.where(position == edge, jnp.zeros((), BF), hid[at, :])

    for r in (0, 1, height - 3, height - 2, height - 1):
        layer_two(r)
    for d in range(2):
        for o in range(own):
            for t in range(tiles):
                out_ref[o, d, :, pl.ds(t * LANES, LANES)] = rows_out[
                    d, t, pl.ds(o, height, stride=own), :
                ].astype(BF)


def one_layer_of_tiles(voxels, first_filters, second_filters):
    n_space, n_chan = lax.axis_size("space"), lax.axis_size("chan")
    c_in, depth, height, width = voxels.shape
    own, c_mid = second_filters.shape[3:]
    sizes = (n_space, n_chan, c_in, own, c_mid, height, width)
    any_space = pl.BlockSpec(memory_space=pl.ANY)
    return pl.pallas_call(
        functools.partial(tile_kernel, sizes),
        out_shape=jax.ShapeDtypeStruct((own, depth, height, width), BF),
        in_specs=[any_space] * 3,
        out_specs=pl.BlockSpec(memory_space=pltpu.VMEM),
        scratch_shapes=[
            pltpu.VMEM(voxels.shape, BF),
            pltpu.VMEM(first_filters.shape, BF),
            pltpu.VMEM(second_filters.shape, BF),
            pltpu.VMEM((2, width // LANES, c_in * height, LANES), F32),
            pltpu.VMEM((2, (height + 5) * c_in, width), BF),
            pltpu.VMEM((n_chan, own, pl.cdiv(27 * c_in, LANES) * LANES), BF),
            pltpu.VMEM((6 * c_mid, 8 * c_in), BF),
            pltpu.VMEM((6 * own, 6 * c_mid), BF),
            pltpu.VMEM(((height + 2) * 2 * c_mid, width), BF),
            pltpu.VMEM((2, width // LANES, height * own, LANES), F32),
            pltpu.SemaphoreType.DMA((3,)),
            pltpu.SemaphoreType.DMA((n_chan + 1,)),
            pltpu.SemaphoreType.DMA((n_chan + 1,)),
        ],
        compiler_params=pltpu.CompilerParams(
            collective_id=0, has_side_effects=True, vmem_limit_bytes=60 * 1024 * 1024
        ),
    )(voxels, first_filters, second_filters)


def solution(mesh):
    return jax.shard_map(
        one_layer_of_tiles if mesh.shape["space"] == GH else local,
        mesh=mesh,
        in_specs=(
            P(None, "space", None, None),
            P(None, None, None, "chan", None),
            P(None, None, None, "chan", None),
        ),
        out_specs=P("chan", "space", None, None),
        check_vma=False,
    )
```
